32 devices in a mesh: frames: 2 (over y), queries: 16 (over z, x, core).
Axes of the slice: x: 2, y: 2, z: 4, core: 2. Of those that a mesh axis runs over, the one named last changes fastest.
Arguments:
- frame_maps: bfloat16 [4, 4096, 256], P('frames', 'queries'), may hold values from -6 to 6
- query_table: bfloat16 [2, 1024, 256], P('frames', 'queries'), may hold values from -6 to 6
- start_frame: int32 [1024], P('queries'), may hold values from 0 to 3
- row_ids: int32 [1024], P('queries'), may hold values from 0 to 63
- conv1_w: bfloat16 [3, 3, 1, 16], replicated, may hold values from -2 to 2
- conv1_b: float32 [16], replicated, may hold values from -3 to 3
- conv2_w: bfloat16 [3, 3, 16, 32], replicated, may hold values from -0.5 to 0.5
- conv2_b: float32 [32], replicated, may hold values from -3 to 3
- proj_w: bfloat16 [32, 512], replicated, may hold values from -1 to 1
- proj_b: float32 [512], replicated, may hold values from -3 to 3
- time_w: float32 [3, 512], replicated, may hold values from -3 to 3
- time_b: float32 [512], replicated, may hold values from -3 to 3
Outputs:
- track_feats: bfloat16 [1024, 4, 512], P('queries', 'frames')
The draws below stay inside these ranges and needn't reach their ends.
Inputs may be any that keep to these rules, and one draw needn't show every extreme that they name: `start_frame`: the frame in which the query was picked, one of the 4 frames. `row_ids`: a row index within the query's own block of 64 rows.
All inputs are finite; a program needn't handle non-finite values.
Results may differ from the reference program's by a relative error of at most 0.001.
The reference program's roundings to bfloat16 on the way count: a program that leaves them out, or rounds other values in their place, can miss the bound.
Values may be sent and summed in bfloat16 or wider, within the bound.
A program may use at most 64 MiB of HBM per device.

```python
import jax
import jax.numpy as jnp
from jax import lax

C = 256
MAP = 64
CH1 = 16
CH2 = 32
D = 512
FR_DEV = 2
Q_DEV = 64
WINDOW = 4
QUERY_ALL = 1024
N_FRAMES = 2


def plant(array, own_key, least, high):
    shape = array.shape
    index_at = [jax.random.randint(jax.random.fold_in(own_key, axis), (), 0, shape[axis]) for axis in range(len(shape))]
    array = array.at[tuple(index_at)].set(least)
    longest = shape.index(max(shape))
    index_at[longest] = (index_at[longest] + 1) % shape[longest]
    return array.at[tuple(index_at)].set(high)


def steps_of(own_key, dims, shards, low, largest):
    def one(position, parts):
        steps = jax.random.uniform(jax.random.fold_in(jax.random.fold_in(own_key, 6), position), (parts,), jnp.float32, low / len(shards), largest / len(shards))
        return jnp.repeat(jnp.exp(steps), dims[position] // parts).reshape((-1,) + (1,) * (len(dims) - position - 1))

    loudness = one(*shards[0])
    for cut in shards[1:]:
        loudness = loudness * one(*cut)
    return loudness


def bell_draw(rng, dims, spread, limit, shards=(), kind=jnp.bfloat16):
    values = jax.random.normal(rng, dims, jnp.float32) * spread
    if len(shards) > 0:
        values = steps_of(rng, dims, shards, -0.22, 0.18) * values
    return jnp.clip(values, min=-limit, max=limit).astype(kind)


def setup_inputs(seed: int = 0) -> dict:
    arg_keys = jax.random.split(jax.random.key(seed), 13)
    frame_maps = bell_draw(arg_keys[0], (WINDOW, MAP * MAP, C), 1.0, 6.0, ((0, 2), (1, 16)))
    query_table = bell_draw(arg_keys[1], (N_FRAMES, QUERY_ALL, C), 1.0, 6.0, ((0, 2), (1, 16)))
    start_frame = plant(jax.random.randint(arg_keys[2], (QUERY_ALL,), 0, WINDOW), jax.random.fold_in(arg_keys[2], 1), 0, WINDOW - 1).astype(jnp.int32)
    row_ids = plant(jax.random.randint(arg_keys[3], (QUERY_ALL,), 0, Q_DEV), jax.random.fold_in(arg_keys[3], 1), 0, Q_DEV - 1).astype(jnp.int32)
    conv1_w = bell_draw(arg_keys[4], (3, 3, 1, CH1), 9 ** -0.5, 2.0)
    conv1_b = bell_draw(arg_keys[5], (CH1,), 0.5, 3.0, (), jnp.float32)
    conv2_w = bell_draw(arg_keys[6], (3, 3, CH1, CH2), (9 * CH1) ** -0.5, 0.5)
    conv2_b = bell_draw(arg_keys[7], (CH2,), 0.5, 3.0, (), jnp.float32)
    proj_w = bell_draw(arg_keys[8], (CH2, D), CH2 ** -0.5, 1.0)
    proj_b = bell_draw(arg_keys[9], (D,), 0.5, 3.0, (), jnp.float32)
    time_w = bell_draw(arg_keys[10], (3, D), 0.6, 3.0, (), jnp.float32)
    time_b = bell_draw(arg_keys[11], (D,), 0.5, 3.0, (), jnp.float32)
    return {"frame_maps": frame_maps, "query_table": query_table, "start_frame": start_frame, "row_ids": row_ids, "conv1_w": conv1_w, "conv1_b": conv1_b, "conv2_w": conv2_w, "conv2_b": conv2_b, "proj_w": proj_w, "proj_b": proj_b, "time_w": time_w, "time_b": time_b}


def cost_block(query_rows, maps_one, conv1_w, conv1_b, conv2_w, conv2_b):
    corr = (jnp.dot(query_rows, maps_one.T, preferred_element_type=jnp.float32) * 0.0625).astype(jnp.bfloat16)
    images = corr.reshape(query_rows.shape[0], 1, MAP, MAP)
    layer_one = lax.conv_general_dilated(images, conv1_w, (2, 2), ((1, 1), (1, 1)), dimension_numbers=("NCHW", "HWIO", "NCHW"), preferred_element_type=jnp.float32)
    layer_one = jax.nn.relu(layer_one + conv1_b[None, :, None, None]).astype(jnp.bfloat16)
    layer_two = lax.conv_general_dilated(layer_one, conv2_w, (2, 2), ((1, 1), (1, 1)), dimension_numbers=("NCHW", "HWIO", "NCHW"), preferred_element_type=jnp.float32)
    layer_two = jax.nn.relu(layer_two + conv2_b[None, :, None, None])
    return jnp.mean(layer_two, axis=(2, 3)).astype(jnp.bfloat16)


def reference(frame_maps, query_table, start_frame, row_ids, conv1_w, conv1_b, conv2_w, conv2_b, proj_w, proj_b, time_w, time_b):
    owner = (start_frame // FR_DEV).astype(jnp.int32)
    table_row = (jnp.arange(QUERY_ALL, dtype=jnp.int32) // Q_DEV * Q_DEV + row_ids).astype(jnp.int32)
    qfeat = query_table[owner, table_row]
    row_block = min(1024, QUERY_ALL)
    query_blocks = qfeat.reshape(QUERY_ALL // row_block, row_block, C)

    def per_frame(maps_one):
        def per_block(query_rows):
            return cost_block(query_rows, maps_one, conv1_w, conv1_b, conv2_w, conv2_b)
        return lax.map(per_block, query_blocks).reshape(QUERY_ALL, CH2)

    pooled = lax.map(per_frame, frame_maps)
    proj = (jnp.dot(pooled.reshape(WINDOW * QUERY_ALL, CH2), proj_w, preferred_element_type=jnp.float32) + proj_b).astype(jnp.bfloat16)
    proj = proj.reshape(WINDOW, QUERY_ALL, D).astype(jnp.float32)
    padded = jnp.pad(proj, ((1, 1), (0, 0), (0, 0)))
    mixed = time_w[0] * padded[:-2] + time_w[1] * padded[1:-1] + time_w[2] * padded[2:] + time_b
    return jnp.transpose(mixed, (1, 0, 2)).astype(jnp.bfloat16)
```

```python
import functools
import math

import jax
import jax.numpy as jnp
from jax import lax
from jax.experimental import pallas as pl
from jax.experimental.pallas import tpu as pltpu
from jax.sharding import PartitionSpec as P

MESH = pl.DeviceIdType.MESH
F32 = jnp.float32
BF16 = jnp.bfloat16


def dot_nn(a, b):
    return jnp.dot(a, b, preferred_element_type=F32)


def dot_nt(a, b):
    return lax.dot_general(a, b, (((1,), (1,)), ((), ())), preferred_element_type=F32)


def dot_tn(a, b):
    return lax.dot_general(a, b, (((0,), (0,)), ((), ())), preferred_element_type=F32)


def column(row):
    n = row.shape[1]
    eye = lax.broadcasted_iota(jnp.int32, (n, n), 0) == lax.broadcasted_iota(jnp.int32, (n, n), 1)
    return jnp.sum(jnp.where(eye, row, 0.0), axis=1, keepdims=True)


def kernel(
    group,
    side,
    maps_ref,
    table_ref,
    start_ref,
    rows_ref,
    w1_ref,
    b1_ref,
    w2_ref,
    b2_ref,
    pw_ref,
    pb_ref,
    tw_ref,
    tb_ref,
    out_ref,
    maps_s,
    own_s,
    qbuf,
    wide1,
    wide2,
    corr_s,
    hid_s,
    part_s,
    sums_s,
    pool_s,
    ex_sem,
    pair_sem,
    halo_sem,
    fwd_sem,
    q_send,
    q_recv,
    p_send,
    p_recv,
    pool_sem,
):
    frames_here, band, _ = maps_ref.shape
    count = table_ref.shape[0]
    ch1 = w1_ref.shape[1]
    ch2 = w2_ref.shape[1]
    halo = 3 * side
    hid_w = side // 2
    out_w = side // 4
    half = out_w // 2
    hid_len = hid_w * ch1
    hid_half = hid_len // 2
    rows = 2 * band // side
    hid_rows = rows // 2 + 1
    out_rows = rows // 4

    f = lax.axis_index("frames")
    me = lax.axis_index("queries")
    core = lax.rem(me, 2)
    k = lax.div(me, 2)
    across = (1 - f, me)
    twin = (f, me + 1 - 2 * core)

    def peer(step):
        return (f, lax.rem(k + step + group, group) * 2 + core)

    barrier = pltpu.get_barrier_semaphore()
    pl.semaphore_signal(barrier, inc=1, device_id=across, device_id_type=MESH)
    pl.semaphore_signal(barrier, inc=1, device_id=twin, device_id_type=MESH)
    for d in range(1, group):
        pl.semaphore_signal(barrier, inc=1, device_id=peer(d), device_id_type=MESH)

    chosen = (lax.broadcasted_iota(jnp.int32, (count, count), 0) == rows_ref[...]) & (
        lax.div(start_ref[...], frames_here) == f
    )
    own_s[0] = dot_tn(jnp.where(chosen, 1.0, 0.0).astype(BF16), table_ref[...]).astype(BF16)
    pl.semaphore_wait(barrier, group + 1)

    def remote(src, dst, send, recv, device):
        return pltpu.make_async_remote_copy(
            src_ref=src, dst_ref=dst, send_sem=send, recv_sem=recv, device_id=device, device_id_type=MESH
        )

    exchange = remote(own_s.at[0], own_s.at[1], ex_sem.at[0], ex_sem.at[1], across)
    exchange.start()
    place = pl.ds(pl.multiple_of(halo + core * band, side), band)
    pairing = remote(maps_ref, maps_s.at[:, place], pair_sem.at[0], pair_sem.at[1], twin)
    pairing.start()
    maps_s[:, place] = maps_ref[...]

    w1 = w1_ref[...]
    tap = lax.broadcasted_iota(jnp.int32, (9, 3 * side), 0)
    cell = lax.broadcasted_iota(jnp.int32, (9, 3 * side), 1)
    tap_row = lax.div(tap, 3)
    tap_at = lax.rem(tap, 3) - 1
    cell_row = lax.div(cell, side)
    cell_at = lax.rem(cell, side)

    def fill1(x, _):
        hit = (tap_row == cell_row) & (cell_at == tap_at + 2 * x)
        spread = jnp.where(hit, 1.0, 0.0).astype(BF16)
        wide1[pl.ds(pl.multiple_of(x * ch1, ch1), ch1), :] = dot_tn(w1, spread).astype(BF16)
        return 0

    lax.fori_loop(0, hid_w, fill1, 0)

    exchange.wait()
    qbuf[0] = own_s[0] + own_s[1]
    q_copies = []
    for d in range(1, group):
        q_copies.append(remote(qbuf.at[0], qbuf.at[d], q_send.at[d], q_recv.at[d], peer(-d)))
        q_copies[-1].start()

    pairing.wait()
    edge = pl.ds(2 * band, halo)
    halo_copy = remote(
        maps_s.at[core, edge], maps_s.at[core, pl.ds(0, halo)], halo_sem.at[0], halo_sem.at[1], peer(1)
    )

    @pl.when(k < group - 1)
    def _():
        halo_copy.start()

    @pl.when(k == 0)
    def _():
        maps_s[:, :halo] = jnp.zeros((frames_here, halo, maps_s.shape[2]), BF16)

    w2 = w2_ref[...]
    taps2 = 3 * ch1
    src = lax.broadcasted_iota(jnp.int32, (taps2, hid_half), 0)
    dst = lax.broadcasted_iota(jnp.int32, (taps2, hid_half), 1)

    def fill2(x, _):
        spread = jnp.where(dst == src + (2 * x - 1) * ch1, 1.0, 0.0).astype(BF16)
        for dy in range(3):
            wide2[pl.ds(pl.multiple_of(x * ch2, ch2), ch2), dy * hid_half : (dy + 1) * hid_half] = dot_tn(
                w2[dy * taps2 : (dy + 1) * taps2], spread
            ).astype(BF16)
        return 0

    lax.fori_loop(0, half, fill2, 0)
    w2_left = jnp.concatenate([w2[dy * taps2 : dy * taps2 + ch1] for dy in range(3)], axis=0)
    b1 = column(b1_ref[...])
    b2 = column(b2_ref[...])

    fwd_copy = remote(
        maps_s.at[core, pl.ds(0, halo)], maps_s.at[core, pl.ds(0, halo)], fwd_sem.at[0], fwd_sem.at[1], twin
    )

    @pl.when(k > 0)
    def _():
        halo_copy.wait_recv()
        fwd_copy.start()
        fwd_copy.wait()

    inner = jnp.where(k > 0, 1.0, 0.0)
    slots = max(s for s in (4, 2, 1) if group % s == 0)
    lanes = slots * count
    p_copies = []
    for chunk in range(group // slots):
        for d in range(chunk * slots, (chunk + 1) * slots):
            if d > 0:
                q_copies[d - 1].wait_recv()
        totals = []
        for frame in range(frames_here):
            queries = qbuf[chunk * slots : (chunk + 1) * slots].reshape(lanes, qbuf.shape[2])
            corr_s[...] = (dot_nt(maps_s[frame], queries) * 0.0625).astype(BF16)
            for r in range(hid_rows):
                h = dot_nn(wide1[...], corr_s[2 * r * side : (2 * r + 3) * side])
                h = jnp.maximum(h.reshape(hid_w, ch1, lanes) + b1, 0.0)
                if r == 0:
                    h = h * inner
                hid_s[r * hid_len : (r + 1) * hid_len] = h.astype(BF16).reshape(hid_len, lanes)
            total = jnp.zeros((ch2, lanes), F32)
            for o in range(out_rows):
                for b in range(2):
                    acc = jnp.zeros((half * ch2, lanes), F32)
                    for dy in range(3):
                        at = (2 * o + dy) * hid_len + b * hid_half
                        acc += dot_nn(
                            wide2[:, dy * hid_half : (dy + 1) * hid_half], hid_s[at : at + hid_half]
                        )
                    if b == 1:
                        left = jnp.concatenate(
                            [
                                hid_s[(2 * o + dy) * hid_len + hid_half - ch1 : (2 * o + dy) * hid_len + hid_half]
                                for dy in range(3)
                            ],
                            axis=0,
                        )
                        acc = jnp.concatenate([acc[:ch2] + dot_tn(w2_left, left), acc[ch2:]], axis=0)
                    total += jnp.sum(jnp.maximum(acc.reshape(half, ch2, lanes) + b2, 0.0), axis=0)
            totals.append(total)
        for i in range(slots):
            d = chunk * slots + i
            part_s[d] = jnp.concatenate([t[:, i * count : (i + 1) * count] for t in totals], axis=1)
            if d > 0:
                p_copies.append(remote(part_s.at[d], sums_s.at[d], p_send.at[d], p_recv.at[d], peer(d)))
                p_copies[-1].start()

    mean = part_s[0]
    for d in range(1, group):
        p_copies[d - 1].wait_recv()
        mean = mean + sums_s[d]
    mean = mean * (1.0 / (out_w * out_w))
    pool_s[0] = mean.astype(BF16)
    pool_copy = remote(pool_s.at[0], pool_s.at[1], pool_sem.at[0], pool_sem.at[1], across)
    pool_copy.start()

    def project(pooled):
        return (dot_tn(pooled, pw_ref[...]) + pb_ref[...]).astype(BF16).astype(F32)

    here = project(pool_s[0])
    first, last = here[:count], here[count:]
    tw = tw_ref[...]
    before, same, after = tw[0:1], tw[1:2], tw[2:3]
    mixed_first = same * first + after * last + tb_ref[...]
    mixed_last = before * first + same * last + tb_ref[...]
    pool_copy.wait()
    there = project(pool_s[1])
    lower = jnp.where(f > 0, there[count:], 0.0)
    upper = jnp.where(f < 1, there[:count], 0.0)
    out_ref[0] = (mixed_first + before * lower).astype(BF16)
    out_ref[1] = (mixed_last + after * upper).astype(BF16)

    for copy in q_copies + p_copies:
        copy.wait_send()

    @pl.when(k < group - 1)
    def _():
        halo_copy.wait_send()


def banded(
    frame_maps, query_table, start_frame, row_ids, conv1_w, conv1_b, conv2_w, conv2_b, proj_w, proj_b, time_w, time_b
):
    frames_here, band, channels = frame_maps.shape
    count = start_frame.shape[0]
    group = lax.axis_size("queries") // 2
    side = math.isqrt(band * group * 2)
    ch1, ch2 = conv2_w.shape[2:]
    width = proj_w.shape[1]
    halo = 3 * side
    cells = halo + 2 * band
    slots = max(s for s in (4, 2, 1) if group % s == 0)
    lanes = slots * count
    hid_len = side // 2 * ch1
    vmem = pl.BlockSpec(memory_space=pltpu.VMEM)
    dma = pltpu.SemaphoreType.DMA
    mixed = pl.pallas_call(
        functools.partial(kernel, group, side),
        out_shape=jax.ShapeDtypeStruct((frames_here, count, width), BF16),
        in_specs=[vmem] * 12,
        out_specs=vmem,
        scratch_shapes=[
            pltpu.VMEM((frames_here, cells, channels), BF16),
            pltpu.VMEM((2, count, channels), BF16),
            pltpu.VMEM((group, count, channels), BF16),
            pltpu.VMEM((hid_len, 3 * side), BF16),
            pltpu.VMEM((side // 8 * ch2, 3 * hid_len // 2), BF16),
            pltpu.VMEM((cells, lanes), BF16),
            pltpu.VMEM(((band // side + 1) * hid_len, lanes), BF16),
            pltpu.VMEM((group, ch2, 2 * count), F32),
            pltpu.VMEM((group, ch2, 2 * count), F32),
            pltpu.VMEM((2, ch2, 2 * count), BF16),
            dma((2,)),
            dma((2,)),
            dma((2,)),
            dma((2,)),
            dma((group,)),
            dma((group,)),
            dma((group,)),
            dma((group,)),
            dma((2,)),
        ],
        compiler_params=pltpu.CompilerParams(
            collective_id=0, has_side_effects=True, vmem_limit_bytes=32 * 1024 * 1024
        ),
    )(
        frame_maps,
        query_table[0],
        start_frame[None],
        row_ids[None],
        conv1_w.reshape(9, ch1),
        conv1_b[None],
        conv2_w.reshape(9 * ch1, ch2),
        conv2_b[None],
        proj_w,
        proj_b[None],
        time_w,
        time_b[None],
    )
    return jnp.transpose(mixed, (1, 0, 2))


MAP = 64
CH2 = 32


def padded(block, sides, width):
    for axis, dim in sides:
        count = lax.axis_size(axis)
        forward = [(i, i + 1) for i in range(count - 1)]
        backward = [(target, source) for source, target in forward]
        low = lax.ppermute(
            lax.slice_in_dim(block, block.shape[dim] - width, None, axis=dim), axis, forward
        )
        high = lax.ppermute(lax.slice_in_dim(block, 0, width, axis=dim), axis, backward)
        block = jnp.concatenate([low, block, high], axis=dim)
    return block


def per_device(
    frame_maps,
    query_table,
    start_frame,
    row_ids,
    conv1_w,
    conv1_b,
    conv2_w,
    conv2_b,
    proj_w,
    proj_b,
    time_w,
    time_b,
):
    frames_here = frame_maps.shape[0]
    frame_block = lax.axis_index("frames")
    own_rows = query_table[0][row_ids]
    owned = start_frame // frames_here == frame_block
    own_term = jnp.where(owned[:, None], own_rows.astype(jnp.float32), 0.0)
    queries = lax.psum(own_term.astype(jnp.bfloat16), "frames")
    query_count = queries.shape[0]
    every_query = lax.all_gather(queries, "queries", axis=0, tiled=True)
    band = (
        jnp.einsum("frc,qc->rfq", frame_maps, every_query, preferred_element_type=jnp.float32)
        * 0.0625
    ).astype(jnp.bfloat16)
    costs = lax.all_to_all(band, "queries", split_axis=2, concat_axis=0, tiled=True)
    block_size = min(64, query_count)
    block_count = query_count // block_size
    pooled_init = jnp.zeros((CH2, frames_here, query_count), jnp.bfloat16)

    def one_block(block_index, pooled_acc):
        images = costs.reshape(MAP, MAP, 1, frames_here * block_size)
        layer_one = lax.conv_general_dilated(
            images,
            conv1_w,
            (2, 2),
            ((1, 1), (1, 1)),
            dimension_numbers=("HWCN", "HWIO", "HWCN"),
            preferred_element_type=jnp.float32,
        )
        layer_one = jax.nn.relu(layer_one + conv1_b[None, None, :, None]).astype(jnp.bfloat16)
        layer_two = lax.conv_general_dilated(
            layer_one,
            conv2_w,
            (2, 2),
            ((1, 1), (1, 1)),
            dimension_numbers=("HWCN", "HWIO", "HWCN"),
            preferred_element_type=jnp.float32,
        )
        layer_two = jax.nn.relu(layer_two + conv2_b[None, None, :, None])
        pooled_block = (
            jnp.mean(layer_two, axis=(0, 1))
            .astype(jnp.bfloat16)
            .reshape(CH2, frames_here, block_size)
        )
        return pooled_block

    pooled = lax.fori_loop(0, block_count, one_block, pooled_init)
    projected = padded(
        (
            jnp.einsum("cfq,cd->qfd", pooled, proj_w, preferred_element_type=jnp.float32) + proj_b
        ).astype(jnp.bfloat16),
        (("frames", 1),),
        1,
    )
    widened_f32 = projected.astype(jnp.float32)
    mixed = (
        time_w[0] * widened_f32[:, :-2]
        + time_w[1] * widened_f32[:, 1:-1]
        + time_w[2] * widened_f32[:, 2:]
        + time_b
    )
    return mixed.astype(jnp.bfloat16)


def solution(mesh):
    placed = (
        P("frames", "queries", None),
        P("frames", "queries", None),
        P("queries"),
        P("queries"),
        P(),
        P(),
        P(),
        P(),
        P(),
        P(),
        P(),
        P(),
    )
    shards = mesh.shape["queries"]

    def chosen(frame_maps, query_table, *rest):
        frames_here, band, _ = frame_maps.shape
        side = math.isqrt(band * shards)
        fits = (
            mesh.shape["frames"] == 2
            and frames_here == 2
            and shards % 2 == 0
            and band % (2 * side) == 0
            and side % 32 == 0
        )
        return (banded if fits else per_device)(frame_maps, query_table, *rest)

    return jax.shard_map(
        chosen,
        mesh=mesh,
        in_specs=placed,
        out_specs=P("queries", "frames", None),
        check_vma=False,
    )
```

```python
import functools
import math

import jax
import jax.numpy as jnp
from jax import lax
from jax.experimental import pallas as pl
from jax.experimental.pallas import tpu as pltpu
from jax.sharding import PartitionSpec as P

MESH = pl.DeviceIdType.MESH
F32 = jnp.float32
BF16 = jnp.bfloat16


def dot_nn(a, b):
    return jnp.dot(a, b, preferred_element_type=F32)


def dot_nt(a, b):
    return lax.dot_general(a, b, (((1,), (1,)), ((), ())), preferred_element_type=F32)


def dot_tn(a, b):
    return lax.dot_general(a, b, (((0,), (0,)), ((), ())), preferred_element_type=F32)


def column(row):
    n = row.shape[1]
    eye = lax.broadcasted_iota(jnp.int32, (n, n), 0) == lax.broadcasted_iota(jnp.int32, (n, n), 1)
    return jnp.sum(jnp.where(eye, row, 0.0), axis=1, keepdims=True)


def kernel(
    group,
    side,
    maps_hbm,
    table_hbm,
    start_hbm,
    rows_hbm,
    w1_hbm,
    b1_hbm,
    w2_hbm,
    b2_hbm,
    pw_hbm,
    pb_hbm,
    tw_hbm,
    tb_hbm,
    out_ref,
    maps_s,
    own_s,
    qbuf,
    wide1,
    wide2,
    corr_s,
    hid_s,
    part_s,
    sums_s,
    pool_s,
    ex_sem,
    pair_sem,
    halo_sem,
    fwd_sem,
    q_send,
    q_recv,
    p_send,
    p_recv,
    pool_sem,
    in_sem,
    *in_refs,
):
    in_hbm = (
        table_hbm, start_hbm, rows_hbm, maps_hbm, w1_hbm, w2_hbm, b1_hbm, b2_hbm, pw_hbm, pb_hbm, tw_hbm, tb_hbm
    )
    loads = [pltpu.make_async_copy(src, dst, in_sem.at[i]) for i, (src, dst) in enumerate(zip(in_hbm, in_refs))]
    for load in loads:
        load.start()
    table_ref, start_ref, rows_ref, maps_ref, w1_ref, w2_ref, b1_ref, b2_ref, pw_ref, pb_ref, tw_ref, tb_ref = in_refs
    frames_here, band, _ = maps_ref.shape
    count = table_ref.shape[0]
    ch1 = w1_ref.shape[2]
    ch2 = w2_ref.shape[1]
    halo = 3 * side
    hid_w = side // 2
    out_w = side // 4
    half = out_w // 2
    hid_len = hid_w * ch1
    hid_half = hid_len // 2
    rows = 2 * band // side
    hid_rows = rows // 2 + 1
    out_rows = rows // 4

    f = lax.axis_index("frames")
    me = lax.axis_index("queries")
    core = lax.rem(me, 2)
    k = lax.div(me, 2)
    across = (1 - f, me)
    twin = (f, me + 1 - 2 * core)

    def peer(step):
        return (f, lax.rem(k + step + group, group) * 2 + core)

    barrier = pltpu.get_barrier_semaphore()
    pl.semaphore_signal(barrier, inc=1, device_id=across, device_id_type=MESH)
    pl.semaphore_signal(barrier, inc=1, device_id=twin, device_id_type=MESH)
    for d in range(1, group):
        pl.semaphore_signal(barrier, inc=1, device_id=peer(d), device_id_type=MESH)

    spill = (core == 1) & (k < group - 1)
    catch = (core == 0) & (k > 0)

    @pl.when(spill)
    def _():
        pl.semaphore_signal(barrier, inc=1, device_id=(f, lax.rem(me + 1, 2 * group)), device_id_type=MESH)

    @pl.when(catch)
    def _():
        pl.semaphore_signal(barrier, inc=1, device_id=(f, lax.rem(me + 2 * group - 1, 2 * group)), device_id_type=MESH)

    for load in loads[:3]:
        load.wait()
    chosen = (lax.broadcasted_iota(jnp.int32, (count, count), 0) == rows_ref[...]) & (
        lax.div(start_ref[...], frames_here) == f
    )
    own_s[0] = dot_tn(jnp.where(chosen, 1.0, 0.0).astype(BF16), table_ref[...]).astype(BF16)
    later = lax.div(2 * group - 2 - k, group)
    earlier = lax.div(k + group - 1, group)
    pl.semaphore_wait(barrier, group + 1 + core * later + (1 - core) * earlier)

    def remote(src, dst, send, recv, device):
        return pltpu.make_async_remote_copy(
            src_ref=src, dst_ref=dst, send_sem=send, recv_sem=recv, device_id=device, device_id_type=MESH
        )

    exchange = remote(own_s.at[0], own_s.at[1], ex_sem.at[0], ex_sem.at[1], across)
    exchange.start()
    loads[3].wait()
    place = pl.ds(pl.multiple_of(halo + core * band, side), band)
    pairing = remote(maps_ref, maps_s.at[:, place], pair_sem.at[0], pair_sem.at[1], twin)
    pairing.start()
    edge = pl.ds(band - halo, halo)
    halo_copies = [
        remote(
            maps_ref.at[c, edge],
            maps_s.at[c, pl.ds(0, halo)],
            halo_sem.at[c],
            halo_sem.at[2],
            (f, lax.rem(k + 1, group) * 2 + c),
        )
        for c in range(2)
    ]

    @pl.when(spill)
    def _():
        for copy in halo_copies:
            copy.start()

    maps_s[:, place] = maps_ref[...]

    exchange.wait()
    qbuf[0] = own_s[0] + own_s[1]
    q_copies = []
    for d in range(1, group):
        q_copies.append(remote(qbuf.at[0], qbuf.at[d], q_send.at[d], q_recv.at[d], peer(-d)))
        q_copies[-1].start()

    @pl.when(k == 0)
    def _():
        maps_s[:, :halo] = jnp.zeros((frames_here, halo, maps_s.shape[2]), BF16)

    for load in loads[4:]:
        load.wait()
    iota = functools.partial(lax.broadcasted_iota, jnp.int32)

    def place_taps(shape, step, at, values):
        offset = lax.rem(lax.div(iota(shape, 2), step), at) - 2 * iota(shape, 0)
        out = jnp.zeros(shape, F32)
        for kx in range(3):
            out = jnp.where(offset == kx - 1, values[kx][None], out)
        return out.astype(BF16)

    tap, cell = iota((3, 3 * side), 0), lax.div(iota((3, 3 * side), 1), side)
    taps1 = []
    for kx in range(3):
        value = jnp.zeros((ch1, 3 * side), F32)
        for dy in range(3):
            spread = jnp.where((tap == kx) & (cell == dy), 1.0, 0.0).astype(BF16)
            value += dot_tn(w1_ref[dy], spread)
        taps1.append(value)
    wide1[...] = place_taps((hid_w, ch1, 3 * side), 1, side, taps1).reshape(hid_len, 3 * side)

    src, dst = iota((3 * ch1, 3 * hid_half), 0), iota((3 * ch1, 3 * hid_half), 1)
    same = (lax.div(src, ch1) == lax.div(dst, hid_half)) & (lax.rem(src, ch1) == lax.rem(dst, ch1))
    spread = jnp.where(same, 1.0, 0.0).astype(BF16)
    w2 = w2_ref[...]
    w2_taps = [
        jnp.concatenate([w2[(3 * dy + kx) * ch1 : (3 * dy + kx + 1) * ch1] for dy in range(3)], axis=0)
        for kx in range(3)
    ]
    taps2 = [dot_tn(w, spread) for w in w2_taps]
    wide2[...] = place_taps((half, ch2, 3 * hid_half), ch1, hid_w // 2, taps2).reshape(half * ch2, 3 * hid_half)
    w2_left = w2_taps[0]
    b1 = column(b1_ref[...])
    b2 = column(b2_ref[...])

    fwd_copy = remote(
        maps_s.at[core, pl.ds(0, halo)], maps_s.at[core, pl.ds(0, halo)], fwd_sem.at[0], fwd_sem.at[1], twin
    )

    pairing.wait()

    @pl.when(k > 0)
    def _():
        halo_copies[0].wait_recv()
        fwd_copy.start()
        fwd_copy.wait()

    inner = jnp.where(k > 0, 1.0, 0.0)
    slots = max(s for s in (4, 2, 1) if group % s == 0)
    lanes = slots * count
    p_copies = []
    for chunk in range(group // slots):
        for d in range(chunk * slots, (chunk + 1) * slots):
            if d > 0:
                q_copies[d - 1].wait_recv()
        totals = []
        for frame in range(frames_here):
            queries = qbuf[chunk * slots : (chunk + 1) * slots].reshape(lanes, qbuf.shape[2])
            corr_s[...] = (dot_nt(maps_s[frame], queries) * 0.0625).astype(BF16)
            for r in range(hid_rows):
                h = dot_nn(wide1[...], corr_s[2 * r * side : (2 * r + 3) * side])
                h = jnp.maximum(h.reshape(hid_w, ch1, lanes) + b1, 0.0)
                if r == 0:
                    h = h * inner
                hid_s[r * hid_len : (r + 1) * hid_len] = h.astype(BF16).reshape(hid_len, lanes)
            total = jnp.zeros((ch2, lanes), F32)
            for o in range(out_rows):
                for b in range(2):
                    acc = jnp.zeros((half * ch2, lanes), F32)
                    for dy in range(3):
                        at = (2 * o + dy) * hid_len + b * hid_half
                        acc += dot_nn(
                            wide2[:, dy * hid_half : (dy + 1) * hid_half], hid_s[at : at + hid_half]
                        )
                    if b == 1:
                        left = jnp.concatenate(
                            [
                                hid_s[(2 * o + dy) * hid_len + hid_half - ch1 : (2 * o + dy) * hid_len + hid_half]
                                for dy in range(3)
                            ],
                            axis=0,
                        )
                        acc = jnp.concatenate([acc[:ch2] + dot_tn(w2_left, left), acc[ch2:]], axis=0)
                    total += jnp.sum(jnp.maximum(acc.reshape(half, ch2, lanes) + b2, 0.0), axis=0)
            totals.append(total)
        for i in range(slots):
            d = chunk * slots + i
            part_s[d] = jnp.concatenate([t[:, i * count : (i + 1) * count] for t in totals], axis=1)
            if d > 0:
                p_copies.append(remote(part_s.at[d], sums_s.at[d], p_send.at[d], p_recv.at[d], peer(d)))
                p_copies[-1].start()

    mean = part_s[0]
    for d in range(1, group):
        p_copies[d - 1].wait_recv()
        mean = mean + sums_s[d]
    mean = mean * (1.0 / (out_w * out_w))
    pool_s[0] = mean.astype(BF16)
    pool_copy = remote(pool_s.at[0], pool_s.at[1], pool_sem.at[0], pool_sem.at[1], across)
    pool_copy.start()

    def project(pooled):
        return (dot_tn(pooled, pw_ref[...]) + pb_ref[...]).astype(BF16).astype(F32)

    here = project(pool_s[0])
    first, last = here[:count], here[count:]
    tw = tw_ref[...]
    before, same, after = tw[0:1], tw[1:2], tw[2:3]
    mixed_first = same * first + after * last + tb_ref[...]
    mixed_last = before * first + same * last + tb_ref[...]
    pool_copy.wait()
    there = project(pool_s[1])
    lower = jnp.where(f > 0, there[count:], 0.0)
    upper = jnp.where(f < 1, there[:count], 0.0)
    out_ref[0] = (mixed_first + before * lower).astype(BF16)
    out_ref[1] = (mixed_last + after * upper).astype(BF16)

    for copy in q_copies + p_copies:
        copy.wait_send()

    @pl.when(spill)
    def _():
        for copy in halo_copies:
            copy.wait_send()


def banded(
    frame_maps, query_table, start_frame, row_ids, conv1_w, conv1_b, conv2_w, conv2_b, proj_w, proj_b, time_w, time_b
):
    frames_here, band, channels = frame_maps.shape
    count = start_frame.shape[0]
    group = lax.axis_size("queries") // 2
    side = math.isqrt(band * group * 2)
    ch1, ch2 = conv2_w.shape[2:]
    width = proj_w.shape[1]
    halo = 3 * side
    cells = halo + 2 * band
    slots = max(s for s in (4, 2, 1) if group % s == 0)
    lanes = slots * count
    hid_len = side // 2 * ch1
    vmem = pl.BlockSpec(memory_space=pltpu.VMEM)
    dma = pltpu.SemaphoreType.DMA
    operands = (
        frame_maps,
        query_table[0],
        start_frame[None],
        row_ids[None],
        conv1_w[:, :, 0],
        conv1_b[None],
        conv2_w.reshape(9 * ch1, ch2),
        conv2_b[None],
        proj_w,
        proj_b[None],
        time_w,
        time_b[None],
    )
    mixed = pl.pallas_call(
        functools.partial(kernel, group, side),
        out_shape=jax.ShapeDtypeStruct((frames_here, count, width), BF16),
        in_specs=[pl.BlockSpec(memory_space=pltpu.HBM)] * 12,
        out_specs=vmem,
        scratch_shapes=[
            pltpu.VMEM((frames_here, cells, channels), BF16),
            pltpu.VMEM((2, count, channels), BF16),
            pltpu.VMEM((group, count, channels), BF16),
            pltpu.VMEM((hid_len, 3 * side), BF16),
            pltpu.VMEM((side // 8 * ch2, 3 * hid_len // 2), BF16),
            pltpu.VMEM((cells, lanes), BF16),
            pltpu.VMEM(((band // side + 1) * hid_len, lanes), BF16),
            pltpu.VMEM((group, ch2, 2 * count), F32),
            pltpu.VMEM((group, ch2, 2 * count), F32),
            pltpu.VMEM((2, ch2, 2 * count), BF16),
            dma((2,)),
            dma((2,)),
            dma((3,)),
            dma((2,)),
            dma((group,)),
            dma((group,)),
            dma((group,)),
            dma((group,)),
            dma((2,)),
            dma((12,)),
            *[pltpu.VMEM(operands[i].shape, operands[i].dtype) for i in (1, 2, 3, 0, 4, 6, 5, 7, 8, 9, 10, 11)],
        ],
        compiler_params=pltpu.CompilerParams(
            collective_id=0, has_side_effects=True, vmem_limit_bytes=60 * 1024 * 1024
        ),
    )(*operands)
    return jnp.transpose(mixed, (1, 0, 2))


MAP = 64
CH2 = 32


def padded(block, sides, width):
    for axis, dim in sides:
        count = lax.axis_size(axis)
        forward = [(i, i + 1) for i in range(count - 1)]
        backward = [(target, source) for source, target in forward]
        low = lax.ppermute(
            lax.slice_in_dim(block, block.shape[dim] - width, None, axis=dim), axis, forward
        )
        high = lax.ppermute(lax.slice_in_dim(block, 0, width, axis=dim), axis, backward)
        block = jnp.concatenate([low, block, high], axis=dim)
    return block


def per_device(
    frame_maps,
    query_table,
    start_frame,
    row_ids,
    conv1_w,
    conv1_b,
    conv2_w,
    conv2_b,
    proj_w,
    proj_b,
    time_w,
    time_b,
):
    frames_here = frame_maps.shape[0]
    frame_block = lax.axis_index("frames")
    own_rows = query_table[0][row_ids]
    owned = start_frame // frames_here == frame_block
    own_term = jnp.where(owned[:, None], own_rows.astype(jnp.float32), 0.0)
    queries = lax.psum(own_term.astype(jnp.bfloat16), "frames")
    query_count = queries.shape[0]
    every_query = lax.all_gather(queries, "queries", axis=0, tiled=True)
    band = (
        jnp.einsum("frc,qc->rfq", frame_maps, every_query, preferred_element_type=jnp.float32)
        * 0.0625
    ).astype(jnp.bfloat16)
    costs = lax.all_to_all(band, "queries", split_axis=2, concat_axis=0, tiled=True)
    block_size = min(64, query_count)
    block_count = query_count // block_size
    pooled_init = jnp.zeros((CH2, frames_here, query_count), jnp.bfloat16)

    def one_block(block_index, pooled_acc):
        images = costs.reshape(MAP, MAP, 1, frames_here * block_size)
        layer_one = lax.conv_general_dilated(
            images,
            conv1_w,
            (2, 2),
            ((1, 1), (1, 1)),
            dimension_numbers=("HWCN", "HWIO", "HWCN"),
            preferred_element_type=jnp.float32,
        )
        layer_one = jax.nn.relu(layer_one + conv1_b[None, None, :, None]).astype(jnp.bfloat16)
        layer_two = lax.conv_general_dilated(
            layer_one,
            conv2_w,
            (2, 2),
            ((1, 1), (1, 1)),
            dimension_numbers=("HWCN", "HWIO", "HWCN"),
            preferred_element_type=jnp.float32,
        )
        layer_two = jax.nn.relu(layer_two + conv2_b[None, None, :, None])
        pooled_block = (
            jnp.mean(layer_two, axis=(0, 1))
            .astype(jnp.bfloat16)
            .reshape(CH2, frames_here, block_size)
        )
        return pooled_block

    pooled = lax.fori_loop(0, block_count, one_block, pooled_init)
    projected = padded(
        (
            jnp.einsum("cfq,cd->qfd", pooled, proj_w, preferred_element_type=jnp.float32) + proj_b
        ).astype(jnp.bfloat16),
        (("frames", 1),),
        1,
    )
    widened_f32 = projected.astype(jnp.float32)
    mixed = (
        time_w[0] * widened_f32[:, :-2]
        + time_w[1] * widened_f32[:, 1:-1]
        + time_w[2] * widened_f32[:, 2:]
        + time_b
    )
    return mixed.astype(jnp.bfloat16)


def solution(mesh):
    placed = (
        P("frames", "queries", None),
        P("frames", "queries", None),
        P("queries"),
        P("queries"),
        P(),
        P(),
        P(),
        P(),
        P(),
        P(),
        P(),
        P(),
    )
    shards = mesh.shape["queries"]

    def chosen(frame_maps, query_table, *rest):
        frames_here, band, _ = frame_maps.shape
        side = math.isqrt(band * shards)
        fits = (
            mesh.shape["frames"] == 2
            and frames_here == 2
            and shards % 2 == 0
            and band % (2 * side) == 0
            and side % 32 == 0
        )
        return (banded if fits else per_device)(frame_maps, query_table, *rest)

    return jax.shard_map(
        chosen,
        mesh=mesh,
        in_specs=placed,
        out_specs=P("queries", "frames", None),
        check_vma=False,
    )
```
